32 devices in a mesh: grp: 2 (over x), tp: 16 (over z, y, core).
Axes of the slice: x: 2, y: 2, z: 4, core: 2. Of those that a mesh axis runs over, the one named last changes fastest.
Arguments:
- activations: bfloat16 [16384, 8192], P('grp', 'tp'), parts along dimension 0, may hold values from -6 to 6
- out_grads: bfloat16 [16384, 28672], P('grp', 'tp'), parts along dimension 0, may hold values from -6 to 6
- proj_in: bfloat16 [8192, 64], P('tp'), may hold values from -0.0625 to 0.0625
- proj_out: bfloat16 [28672, 64], P('tp'), may hold values from -0.03125 to 0.03125
- seg_ids: int32 [16384], P('grp'), parts along dimension 0, may hold values from 0 to 7, never falling along the last dimension, each value on 1 to 4096 neighbouring positions
- queries: float32 [1024, 4096], P('tp'), may hold values from -6 to 6
Outputs:
- scores: float32 [16, 1024], P('grp', 'tp'), parts along dimension 0
The draws below stay inside these ranges and needn't reach their ends.
There are 2 independent parts, one for each index of `grp`. The reference program is written for one: setup_inputs(seed, part) draws one part's arguments, and reference() takes and returns one part's arrays. A program takes and returns all parts, laid end to end along the dimension named above; an argument that names none is the same for every part. Nothing has to cross between parts.
Inputs may be any that keep to these rules, and one draw needn't show every extreme that they name: `seg_ids`: never falling along the tokens; every sequence has one token or more, and one has exactly 4096.
All inputs are finite; a program needn't handle non-finite values.
Results may differ from the reference program's by a relative error of at most 0.0003.
Values sent between devices are 32-bit elements; how exact they have to be, the bound alone decides.
No kernel may reach another device: no remote copies, remote signals or barrier semaphores. Data moves between devices by JAX's collectives and lax.ppermute only.
A program may use at most 128 MiB of HBM per device.

```python
import math
import jax
import jax.numpy as jnp
import numpy as np
from jax import lax

D = 8192
FF = 28672
RANK = 64
TOKENS = 8192
SEQS = 8
NQ = 1024


def spiked(values, key, source, target, shards_of, factor):
    owner, partner = [(jnp.arange(values.shape[position]) // (values.shape[position] // shards_of)).reshape([-1 if axis == position else 1 for axis in range(values.ndim)]) for position in (source, target)]
    chosen = jax.random.permutation(key, shards_of)[partner]
    strong = (owner == chosen) | (owner == (partner + shards_of // 2) % shards_of)
    return jnp.where(strong, factor * values, values)


def block_levels(rng, dims, split, least, largest):
    loudness, own = 1.0, jax.random.fold_in(rng, 6)
    for dim, shards_of in split:
        steps = jnp.exp(jax.random.uniform(jax.random.fold_in(own, dim), (shards_of,), jnp.float32, least / len(split), largest / len(split)))
        loudness = loudness * jnp.repeat(steps, dims[dim] // shards_of).reshape([-1 if axis == dim else 1 for axis in range(len(dims))])
    return loudness


def split_up(count, total, most, skew):
    weights = [(1 << 20) // math.isqrt(standing ** skew) + 1 for standing in range(2, count + 1)]
    spare, given = total - most - (count - 1), [1] * (count - 1)
    while spare > 0:
        candidates = [i for i in range(count - 1) if given[i] < most]
        mass, budget = sum([weights[i] for i in candidates]), spare
        for i in candidates:
            addition = min(most - given[i], max(1, budget * weights[i] // mass), spare)
            given[i] = given[i] + addition
            spare = spare - addition
    return np.array([most] + given)


def ragged_sizes(key, number_of, total, most, lean):
    if number_of == 2:
        one = jax.random.randint(key, (), max(1, total - most), min(most, total - 1) + 1)
        return jnp.stack([one, total - one])
    sizes = jnp.asarray(split_up(number_of, total, most, lean), jnp.int32)
    twos = (number_of - 1) // 2
    source_of, receiver = sizes[1:1 + 2 * twos:2], sizes[2:2 + 2 * twos:2]
    slack = jnp.minimum(source_of - 1, most - receiver)
    passed = jax.random.randint(jax.random.fold_in(key, 1), (twos,), 0, 1 << 20) % (slack + 1)
    sizes = sizes.at[1:1 + 2 * twos:2].set(source_of - passed).at[2:2 + 2 * twos:2].set(receiver + passed)
    return sizes[jax.random.permutation(jax.random.fold_in(key, 2), number_of)]


def scatter_about(key, shape, scale, bound, cuts=(), held_as=jnp.bfloat16):
    level = block_levels(key, shape, cuts, -0.22, 0.18) if cuts else 1.0
    entries = jax.random.normal(key, shape, jnp.float32) * scale * level
    return jnp.minimum(jnp.maximum(entries, -bound), bound).astype(held_as)


def heavy_noise(key, extent, deviation, bound, split, heavy, kind=jnp.bfloat16):
    drawn = deviation * jax.random.normal(key, extent, jnp.float32)
    if split:
        drawn = drawn * block_levels(key, extent, split, -0.22, 0.18)
    return jnp.clip(spiked(drawn, jax.random.fold_in(key, 3), *heavy), -bound, bound).astype(kind)


def setup_inputs(seed: int = 0, part: int = 0) -> dict:
    keys = jax.random.split(jax.random.key(seed), 7)
    own_keys = jax.random.split(jax.random.fold_in(keys[6], part), 7)
    activations = heavy_noise(own_keys[0], (TOKENS, D), 1.0, 6.0, ((1, 16),), (1, 0, 16, 2.0))
    out_grads = heavy_noise(own_keys[1], (TOKENS, FF), 1.0, 6.0, ((1, 16),), (1, 0, 16, 2.0))
    proj_in = scatter_about(keys[2], (D, RANK), D ** -0.5, 0.0625, ((0, 16),))
    proj_out = scatter_about(keys[3], (FF, RANK), FF ** -0.5, 0.03125, ((0, 16),))
    seg_ids = jnp.searchsorted(jnp.cumsum(ragged_sizes(own_keys[4], SEQS, TOKENS, TOKENS // 2, 0)), jnp.arange(TOKENS), side="right").astype(jnp.int32)
    queries = scatter_about(keys[5], (NQ, RANK * RANK), 1.0, 6.0, ((0, 16),), jnp.float32)
    return dict(activations=activations, out_grads=out_grads, proj_in=proj_in, proj_out=proj_out, seg_ids=seg_ids, queries=queries)


def reference(activations, out_grads, proj_in, proj_out, seg_ids, queries):
    proj_x = jnp.dot(activations, proj_in, preferred_element_type=jnp.float32)
    proj_g = jnp.dot(out_grads, proj_out, preferred_element_type=jnp.float32)
    onehot = (seg_ids[:, None] == jnp.arange(SEQS, dtype=jnp.int32)[None, :]).astype(jnp.float32)
    counts = jnp.sum(onehot, axis=0)
    weighted = (onehot[:, :, None] * proj_g[:, None, :]).reshape(TOKENS, SEQS * RANK)
    seq_grads = jnp.dot(weighted.T, proj_x, precision=lax.Precision.HIGHEST, preferred_element_type=jnp.float32)
    seq_grads = seq_grads.reshape(SEQS, RANK * RANK) / counts[:, None]
    return jnp.dot(seq_grads, queries.T, precision=lax.Precision.HIGHEST, preferred_element_type=jnp.float32)
```

```python
import functools

import jax
import jax.numpy as jnp
from jax import lax
from jax.experimental import pallas as pl
from jax.experimental.pallas import tpu as pltpu
from jax.sharding import PartitionSpec as P

SEQS = 8
CHUNKS = 4
STEPS = 4


def project_kernel(low_bits, me_ref, a_ref, g_ref, pi_ref, po_ref, send_ref, keep_ref):
    step = pl.program_id(0)
    count = 1 << low_bits
    low = me_ref[0] & (count - 1)
    rows = a_ref.shape[0] // count
    side_x = jnp.dot(a_ref[...], pi_ref[...], preferred_element_type=jnp.float32)
    side_g = jnp.dot(g_ref[...], po_ref[...], preferred_element_type=jnp.float32)
    both = jnp.concatenate([side_x, side_g], axis=1)

    def store(out_ref):
        for part in range(count):
            start = pl.multiple_of((part ^ low) * rows, rows)
            out_ref[pl.ds(start, rows), :] = both[part * rows : (part + 1) * rows]

    @pl.when(step < STEPS // 2)
    def _():
        store(send_ref)

    @pl.when(step >= STEPS // 2)
    def _():
        store(keep_ref)


def project(chunk, bits, me_rev, activations, out_grads, proj_in, proj_out):
    tokens, width = activations.shape
    hidden = out_grads.shape[1]
    rank = proj_in.shape[1]
    rows = tokens // CHUNKS // STEPS
    low_bits = bits - 2
    half = STEPS // 2

    def source(j, me):
        return (chunk * STEPS + (((j + half) % STEPS) ^ (me[0] >> low_bits)), 0)

    out = jax.ShapeDtypeStruct((tokens // CHUNKS // 2, 2 * rank), jnp.float32)
    return pl.pallas_call(
        functools.partial(project_kernel, low_bits),
        grid_spec=pltpu.PrefetchScalarGridSpec(
            num_scalar_prefetch=1,
            grid=(STEPS,),
            in_specs=[
                pl.BlockSpec((rows, width), source),
                pl.BlockSpec((rows, hidden), source),
                pl.BlockSpec((width, rank), lambda j, me: (0, 0)),
                pl.BlockSpec((hidden, rank), lambda j, me: (0, 0)),
            ],
            out_specs=[
                pl.BlockSpec((rows, 2 * rank), lambda j, me: (jnp.minimum(j, half - 1), 0)),
                pl.BlockSpec((rows, 2 * rank), lambda j, me: (jnp.maximum(j - half, 0), 0)),
            ],
        ),
        out_shape=[out, out],
        compiler_params=pltpu.CompilerParams(vmem_limit_bytes=32 * 1024 * 1024),
        cost_estimate=pl.CostEstimate(
            flops=2 * rows * STEPS * (width + hidden) * rank,
            bytes_accessed=2 * rows * STEPS * (width + hidden),
            transcendentals=0,
        ),
        name="project",
    )(me_rev, activations, out_grads, proj_in, proj_out)


def product_kernel(seq_count, terms_ref, seg_ref, scale_ref, out_ref):
    terms = terms_ref[...]
    rank = terms.shape[1] // 2
    proj_x = terms[:, :rank]
    proj_g = terms[:, rank:]
    seg = seg_ref[...]
    x_hi = proj_x.astype(jnp.bfloat16)
    x_lo = (proj_x - x_hi.astype(jnp.float32)).astype(jnp.bfloat16)
    g_hi = proj_g.astype(jnp.bfloat16)
    g_lo = (proj_g - g_hi.astype(jnp.float32)).astype(jnp.bfloat16)
    x_both = jnp.concatenate([x_hi, x_lo], axis=1)
    g_both = jnp.concatenate([g_hi, g_lo], axis=1)
    half = rank // 2
    for s in range(seq_count):
        masked = jnp.where(seg == s, g_both, jnp.zeros_like(g_both))
        quad = lax.dot_general(
            masked, x_both, (((0,), (0,)), ((), ())), preferred_element_type=jnp.float32
        )
        total = (
            quad[:rank, :rank] + quad[rank:, :rank] + (quad[:rank, rank:] + quad[rank:, rank:])
        ) * scale_ref[s]
        out_ref[s * rank : (s + 1) * rank, :] = total


def product(terms, seg_rows, scale, seq_count):
    rows, width = terms.shape
    rank = width // 2
    return pl.pallas_call(
        functools.partial(product_kernel, seq_count),
        in_specs=[
            pl.BlockSpec(memory_space=pltpu.VMEM),
            pl.BlockSpec(memory_space=pltpu.VMEM),
            pl.BlockSpec(memory_space=pltpu.SMEM),
        ],
        out_specs=pl.BlockSpec(memory_space=pltpu.VMEM),
        out_shape=jax.ShapeDtypeStruct((seq_count * rank, rank), jnp.float32),
        compiler_params=pltpu.CompilerParams(vmem_limit_bytes=32 * 1024 * 1024),
        name="product",
    )(terms, seg_rows, scale)


def shards(devices, activations, out_grads, proj_in, proj_out, seg_ids, queries):
    bits = devices.bit_length() - 1
    tokens = activations.shape[0]
    rank = proj_in.shape[1]
    me = lax.axis_index("tp")
    me_rev = jnp.int32(0)
    for b in range(bits):
        me_rev = me_rev | (((me >> b) & 1) << (bits - 1 - b))

    def swap(value, bit):
        return lax.ppermute(value, "tp", [(i, i ^ (1 << bit)) for i in range(devices)])

    counts = jnp.sum(
        (seg_ids[None, :] == jnp.arange(SEQS, dtype=jnp.int32)[:, None]).astype(jnp.float32), axis=1
    )
    scale = 1.0 / counts
    own = tokens // CHUNKS // devices
    seg_own = lax.dynamic_slice_in_dim(
        seg_ids.reshape(CHUNKS, devices, own), me_rev, 1, axis=1
    ).reshape(CHUNKS * own)
    seg_rows = jnp.broadcast_to(seg_own[:, None], (CHUNKS * own, 2 * rank))

    done = []
    for chunk in range(CHUNKS):
        send, keep = project(
            chunk, bits, me_rev.reshape(1), activations, out_grads, proj_in, proj_out
        )
        for b in range(bits):
            received = swap(send, b)
            half = keep.shape[0] // 2
            if b < bits - 1:
                send = keep[half:] + received[half:]
                keep = keep[:half] + received[:half]
            else:
                keep = keep + received
        done.append(keep)
    terms = jnp.concatenate(done, axis=0)
    grads = product(terms, seg_rows, scale, SEQS).reshape(SEQS, rank * rank)
    for b in range(bits):
        grads = grads + swap(grads, b)
    return jnp.dot(
        grads, queries.T, precision=lax.Precision.HIGHEST, preferred_element_type=jnp.float32
    )


def solution(mesh):
    placed = (P("grp", "tp"), P("grp", "tp"), P("tp", None), P("tp", None), P("grp"), P("tp", None))
    return jax.shard_map(
        functools.partial(shards, mesh.shape["tp"]),
        mesh=mesh,
        in_specs=placed,
        out_specs=P("grp", "tp"),
        check_vma=False,
    )
```

```python
import functools

import jax
import jax.numpy as jnp
from jax import lax
from jax.experimental import pallas as pl
from jax.experimental.pallas import tpu as pltpu
from jax.sharding import PartitionSpec as P

SEQS = 8
UNITS = 16
CHUNKS = (2, 4, 4, 4, 2)
BOTH_SIDES = 1
BLOCK = 256
VMEM = 56 * 1024 * 1024
ROWS_BY_ROWS = (((1,), (1,)), ((), ()))


def project_kernel(first, rows, blocks, low_bits, me_ref, a_hbm, g_hbm, pi_ref, po_ref, send_ref, keep_ref, a_buf, g_buf, sems):
    size = rows // blocks
    count = 1 << low_bits
    part_rows = size // count
    high = me_ref[0] >> low_bits
    low = me_ref[0] & (count - 1)
    half = blocks // 2
    order = list(range(half, blocks)) + list(range(half))

    def copies(slot):
        start = pl.multiple_of(first + (order[slot] ^ high) * size, 16)
        held = pl.ds(slot * size, size)
        return (
            pltpu.make_async_copy(a_hbm.at[pl.ds(start, size), :], a_buf.at[held, :], sems.at[slot, 0]),
            pltpu.make_async_copy(g_hbm.at[pl.ds(start, size), :], g_buf.at[held, :], sems.at[slot, 1]),
        )

    for slot in range(blocks):
        for copy in copies(slot):
            copy.start()
    for slot in range(blocks):
        for copy in copies(slot):
            copy.wait()
        held = slice(slot * size, (slot + 1) * size)
        side_x = lax.dot_general(a_buf[held, :], pi_ref[...], ROWS_BY_ROWS, preferred_element_type=jnp.float32)
        side_g = lax.dot_general(g_buf[held, :], po_ref[...], ROWS_BY_ROWS, preferred_element_type=jnp.float32)
        both = jnp.concatenate([side_x, side_g], axis=1)
        out_ref = send_ref if slot < half else keep_ref
        base = (slot % half) * size
        for part in range(count):
            start = pl.multiple_of(base + (part ^ low) * part_rows, 8)
            out_ref[pl.ds(start, part_rows), :] = both[part * part_rows : (part + 1) * part_rows]


def project(first, rows, bits, me_rev, activations, out_grads, proj_in, proj_out):
    width = activations.shape[1]
    hidden = out_grads.shape[1]
    rank = proj_in.shape[0]
    block_bits = max(1, (-(-rows // BLOCK) - 1).bit_length())
    blocks = 1 << block_bits
    out = jax.ShapeDtypeStruct((rows // 2, 2 * rank), jnp.float32)
    vmem = pl.BlockSpec(memory_space=pltpu.VMEM)
    return pl.pallas_call(
        functools.partial(project_kernel, first, rows, blocks, bits - block_bits),
        in_specs=[
            pl.BlockSpec(memory_space=pltpu.SMEM),
            pl.BlockSpec(memory_space=pl.ANY),
            pl.BlockSpec(memory_space=pl.ANY),
            vmem,
            vmem,
        ],
        out_specs=[vmem, vmem],
        out_shape=[out, out],
        scratch_shapes=[
            pltpu.VMEM((rows, width), activations.dtype),
            pltpu.VMEM((rows, hidden), out_grads.dtype),
            pltpu.SemaphoreType.DMA((blocks, 2)),
        ],
        compiler_params=pltpu.CompilerParams(vmem_limit_bytes=VMEM),
        cost_estimate=pl.CostEstimate(
            flops=2 * rows * (width + hidden) * rank,
            bytes_accessed=2 * rows * (width + hidden),
            transcendentals=0,
        ),
        name="project",
    )(me_rev, activations, out_grads, proj_in, proj_out)


def product_kernel(pieces, bits, me_ref, edge_ref, scale_ref, *refs):
    term_refs = refs[: len(pieces)]
    send_ref, keep_ref, held_ref = refs[len(pieces) :]
    terms = jnp.concatenate([ref[...] for ref in term_refs], axis=0)
    total_rows = terms.shape[0]
    rank = terms.shape[1] // 2
    me = me_ref[0]
    lane = lax.broadcasted_iota(jnp.int32, (1, total_rows), 1)
    token = lane
    offset = 0
    for first, rows, count in pieces:
        for part in range(count):
            start = first + (me ^ part) * rows
            token = jnp.where(lane >= offset, lane + (start - offset), token)
            offset += rows
    proj_x = terms[:, :rank]
    x_hi = proj_x.astype(jnp.bfloat16)
    x_lo = (proj_x - x_hi.astype(jnp.float32)).astype(jnp.bfloat16)
    x_both = jnp.concatenate([x_hi, x_lo], axis=1)
    g_rows = terms.T[rank:, :]
    half = rank // 2
    side = me >> (bits - 1)
    group = SEQS // 2
    for place in range(SEQS):
        s = place ^ (side * group)
        inside = (token >= edge_ref[s]) & (token < edge_ref[s + 1])
        masked = jnp.where(inside, g_rows, 0.0)
        g_hi = masked.astype(jnp.bfloat16)
        g_lo = (masked - g_hi.astype(jnp.float32)).astype(jnp.bfloat16)
        quad = jnp.dot(jnp.concatenate([g_hi, g_lo], axis=0), x_both, preferred_element_type=jnp.float32)
        small = quad[rank:, rank:] + (quad[rank:, :rank] + quad[:rank, rank:])
        total = (quad[:rank, :rank] + small) * scale_ref[s]
        held_ref[place, :, :rank] = total
        even = held_ref[place, pl.ds(0, half, stride=2), :]
        odd = held_ref[place, pl.ds(1, half, stride=2), :]
        out_ref = keep_ref if place < group else send_ref
        row = (place % group) * half
        out_ref[row : row + half, :] = jnp.concatenate([even[:, :rank], odd[:, :rank]], axis=1)


def product(pieces, bits, me_rev, edges, scale, terms):
    rank = terms[0].shape[1] // 2
    out = jax.ShapeDtypeStruct((SEQS // 2 * rank // 2, 2 * rank), jnp.float32)
    vmem = pl.BlockSpec(memory_space=pltpu.VMEM)
    smem = pl.BlockSpec(memory_space=pltpu.SMEM)
    return pl.pallas_call(
        functools.partial(product_kernel, pieces, bits),
        in_specs=[smem, smem, smem] + [vmem] * len(terms),
        out_specs=[vmem, vmem],
        out_shape=[out, out],
        scratch_shapes=[pltpu.VMEM((SEQS, rank, 2 * rank), jnp.float32)],
        compiler_params=pltpu.CompilerParams(vmem_limit_bytes=VMEM),
        name="product",
    )(me_rev, edges, scale, *terms)


def score_kernel(side_ref, mine_ref, other_ref, q_ref, out_ref):
    queries, depth = q_ref.shape
    lanes = mine_ref.shape[1]
    columns = depth // lanes
    group = SEQS // 2
    step = 16
    rows = [[] for _ in range(SEQS)]
    for start in range(0, queries, step):
        sums = [jnp.zeros((step, lanes), jnp.float32) for _ in range(SEQS)]
        for column in range(columns):
            block = q_ref[start : start + step, column * lanes : (column + 1) * lanes]
            for s in range(SEQS):
                ref = mine_ref if s < group else other_ref
                row = (s % group) * columns + column
                sums[s] = sums[s] + block * ref[row : row + 1, :]
        for s in range(SEQS):
            rows[s].append(sums[s])
    lines = [jnp.sum(jnp.concatenate(parts, axis=0).T, axis=0, keepdims=True) for parts in rows]
    plain = jnp.concatenate(lines, axis=0)
    turned = jnp.concatenate(lines[group:] + lines[:group], axis=0)
    out_ref[...] = jnp.where(side_ref[0] == 0, plain, turned)


def score(side, mine, other, queries):
    vmem = pl.BlockSpec(memory_space=pltpu.VMEM)
    return pl.pallas_call(
        score_kernel,
        in_specs=[pl.BlockSpec(memory_space=pltpu.SMEM), vmem, vmem, vmem],
        out_specs=vmem,
        out_shape=jax.ShapeDtypeStruct((SEQS, queries.shape[0]), jnp.float32),
        compiler_params=pltpu.CompilerParams(vmem_limit_bytes=VMEM),
        name="score",
    )(side, mine, other, queries)


def shards(devices, activations, out_grads, proj_in, proj_out, seg_ids, queries):
    bits = devices.bit_length() - 1
    last = bits - 1
    tokens = activations.shape[0]
    unit = tokens // UNITS
    me = lax.axis_index("tp").astype(jnp.int32)
    me_rev = jnp.int32(0)
    for b in range(bits):
        me_rev = me_rev | (((me >> b) & 1) << (bits - 1 - b))
    me_rev = me_rev.reshape(1)
    weights_in, weights_out = proj_in.T, proj_out.T

    def swap(value, bit):
        return lax.ppermute(value, "tp", [(i, i ^ (1 << bit)) for i in range(devices)])

    edges = jnp.sum(
        (seg_ids[None, :] < jnp.arange(SEQS + 1, dtype=jnp.int32)[:, None]).astype(jnp.int32), axis=1
    )
    scale = 1.0 / (edges[1:] - edges[:-1]).astype(jnp.float32)

    tie = me_rev
    sums = []
    early, late = [], []
    for k, share in enumerate(CHUNKS):
        rows = share * unit
        first = sum(CHUNKS[:k]) * unit
        if k > 0:
            tie, _ = lax.optimization_barrier((me_rev, sums[max(0, k - 1 if k < 3 else k - 2)]))
        send, keep = project(first, rows, bits, tie, activations, out_grads, weights_in, weights_out)
        on_both = k >= len(CHUNKS) - BOTH_SIDES
        for b in range(bits):
            if b == last and on_both:
                half = keep.shape[0] // 2
                whole = jnp.concatenate([keep, send], axis=0)
                turned = swap(jnp.concatenate([send, keep], axis=0), b)
                keep = whole + turned
            else:
                received = swap(send, b)
                if b < last:
                    half = keep.shape[0] // 2
                    send = keep[half:] + received[half:]
                    keep = keep[:half] + received[:half]
                else:
                    keep = keep + received
            if b == 0:
                sums.append(send)
        (late if on_both else early).append((keep, (first, rows // devices, 2 if on_both else 1)))

    def group_product(group):
        return product(tuple(p for _, p in group), bits, me_rev, edges, scale, [t for t, _ in group])

    send, keep = group_product(early)
    grads = keep + swap(send, 0)
    grads = grads + swap(grads, last)
    send, keep = group_product(late)
    grads = grads + keep + swap(send, 0)
    for b in range(1, last):
        grads = grads + swap(grads, b)
    return score(me_rev >> last, grads, swap(grads, 0), queries)


def solution(mesh):
    placed = (P("grp", "tp"), P("grp", "tp"), P("tp", None), P("tp", None), P("grp"), P("tp", None))
    return jax.shard_map(
        functools.partial(shards, mesh.shape["tp"]),
        mesh=mesh,
        in_specs=placed,
        out_specs=P("grp", "tp"),
        check_vma=False,
    )
```

```python
import functools

import jax
import jax.numpy as jnp
from jax import lax
from jax.experimental import pallas as pl
from jax.experimental.pallas import tpu as pltpu
from jax.sharding import PartitionSpec as P

SEQS = 8
UNITS = 16
CHUNKS = (4, 4, 4, 3, 1)
BOTH_SIDES = 2
BLOCK = 512
VMEM = 48 * 1024 * 1024
ROWS_BY_ROWS = (((1,), (1,)), ((), ()))


def project_kernel(bits, block_bits, shares, a_hbm, g_hbm, pi_hbm, po_hbm, *refs):
    outs, (pi_ref, po_ref, a_buf, g_buf, sems) = refs[:-5], refs[-5:]
    ring, size = a_buf.shape[0], a_buf.shape[1]
    blocks = 1 << block_bits
    count = 1 << (bits - block_bits)
    own = size // count
    half = blocks // 2
    me_rev = reversed_index(bits)
    high = me_rev >> (bits - block_bits)
    low = me_rev & (count - 1)

    def copies(step):
        slot = lax.rem(step, ring)
        start = pl.multiple_of((step ^ high) * size, size)
        return (
            pltpu.make_async_copy(a_hbm.at[pl.ds(start, size), :], a_buf.at[slot], sems.at[slot, 0]),
            pltpu.make_async_copy(g_hbm.at[pl.ds(start, size), :], g_buf.at[slot], sems.at[slot, 1]),
        )

    weights = (
        pltpu.make_async_copy(pi_hbm, pi_ref, sems.at[ring, 0]),
        pltpu.make_async_copy(po_hbm, po_ref, sems.at[ring, 1]),
    )
    for copy in weights:
        copy.start()
    for step in range(min(ring - 1, blocks)):
        for copy in copies(jnp.int32(step)):
            copy.start()
    for copy in weights:
        copy.wait()

    def body(step, carry):
        @pl.when(step + ring - 1 < blocks)
        def _():
            for copy in copies(step + ring - 1):
                copy.start()

        for copy in copies(step):
            copy.wait()
        slot = lax.rem(step, ring)
        side_x = lax.dot_general(a_buf[slot], pi_ref[...], ROWS_BY_ROWS, preferred_element_type=jnp.float32)
        side_g = lax.dot_general(g_buf[slot], po_ref[...], ROWS_BY_ROWS, preferred_element_type=jnp.float32)
        both = jnp.concatenate([side_x, side_g], axis=1)
        base = (step & (half - 1)) * count

        def store(out_refs):
            for part in range(count):
                place = base + (part ^ low)
                row = part * own
                for share, out_ref in zip(shares, out_refs, strict=True):
                    start = pl.multiple_of(place * share, 8)
                    out_ref[pl.ds(start, share), :] = both[row : row + share]
                    row += share

        @pl.when(step < half)
        def _():
            store(outs[1::2])

        @pl.when(step >= half)
        def _():
            store(outs[0::2])

        return carry

    lax.fori_loop(0, blocks, body, 0)


def reversed_index(bits):
    me = lax.axis_index("tp").astype(jnp.int32)
    flipped = jnp.int32(0)
    for b in range(bits):
        flipped = flipped | (((me >> b) & 1) << (bits - 1 - b))
    return flipped


def project(bits, shares, activations, out_grads, proj_in, proj_out):
    tokens, width = activations.shape
    hidden = out_grads.shape[1]
    rank = proj_in.shape[0]
    block_bits = min(bits, max(2, (tokens // BLOCK - 1).bit_length()))
    size = tokens >> block_bits
    ring = 4
    outs = [
        jax.ShapeDtypeStruct(((1 << bits) // 2 * share, 2 * rank), jnp.float32)
        for share in shares
        for _ in range(2)
    ]
    vmem = pl.BlockSpec(memory_space=pltpu.VMEM)
    return pl.pallas_call(
        functools.partial(project_kernel, bits, block_bits, shares),
        in_specs=[pl.BlockSpec(memory_space=pl.ANY)] * 4,
        out_specs=[vmem] * len(outs),
        out_shape=outs,
        scratch_shapes=[
            pltpu.VMEM(proj_in.shape, proj_in.dtype),
            pltpu.VMEM(proj_out.shape, proj_out.dtype),
            pltpu.VMEM((ring, size, width), activations.dtype),
            pltpu.VMEM((ring, size, hidden), out_grads.dtype),
            pltpu.SemaphoreType.DMA((ring + 1, 2)),
        ],
        compiler_params=pltpu.CompilerParams(vmem_limit_bytes=VMEM),
        name="project",
    )(activations, out_grads, proj_in, proj_out)


def product_kernel(pieces, bits, own, edge_ref, scale_ref, *refs):
    term_refs = refs[: len(pieces)]
    send_ref, keep_ref, held_ref = refs[len(pieces) :]
    terms = jnp.concatenate([ref[...] for ref in term_refs], axis=0)
    total_rows = terms.shape[0]
    rank = terms.shape[1] // 2
    me = reversed_index(bits)
    lane = lax.broadcasted_iota(jnp.int32, (1, total_rows), 1)
    token = lane
    offset = 0
    for first, rows, count in pieces:
        for part in range(count):
            start = (me ^ part) * own + first
            token = jnp.where(lane >= offset, lane + (start - offset), token)
            offset += rows
    proj_x = terms[:, :rank]
    x_hi = proj_x.astype(jnp.bfloat16)
    x_lo = (proj_x - x_hi.astype(jnp.float32)).astype(jnp.bfloat16)
    x_both = jnp.concatenate([x_hi, x_lo], axis=1)
    g_rows = terms.T[rank:, :]
    half = rank // 2
    side = me >> (bits - 1)
    group = SEQS // 2
    places = [place ^ (side * group) for place in range(SEQS)]
    high_parts, low_parts = [], []
    for s in places:
        inside = (token >= edge_ref[s]) & (token < edge_ref[s + 1])
        masked = jnp.where(inside, g_rows, 0.0)
        g_hi = masked.astype(jnp.bfloat16)
        high_parts.append(g_hi)
        low_parts.append((masked - g_hi.astype(jnp.float32)).astype(jnp.bfloat16))
    g_both = jnp.concatenate(high_parts + low_parts, axis=0)
    quad = jnp.dot(g_both, x_both, preferred_element_type=jnp.float32)
    upper, lower = quad[: SEQS * rank], quad[SEQS * rank :]
    total = upper[:, :rank] + (upper[:, rank:] + lower[:, :rank] + lower[:, rank:])
    for place, s in enumerate(places):
        rows = slice(place * rank, (place + 1) * rank)
        held_ref[rows, :rank] = total[rows] * scale_ref[s]
    even = held_ref[pl.ds(0, SEQS * half, stride=2), :]
    odd = held_ref[pl.ds(1, SEQS * half, stride=2), :]
    packed = jnp.concatenate([even[:, :rank], odd[:, :rank]], axis=1)
    keep_ref[...] = packed[: group * half]
    send_ref[...] = packed[group * half :]


def product(pieces, bits, own, edges, scale, terms):
    rank = terms[0].shape[1] // 2
    out = jax.ShapeDtypeStruct((SEQS // 2 * rank // 2, 2 * rank), jnp.float32)
    vmem = pl.BlockSpec(memory_space=pltpu.VMEM)
    smem = pl.BlockSpec(memory_space=pltpu.SMEM)
    return pl.pallas_call(
        functools.partial(product_kernel, pieces, bits, own),
        in_specs=[smem, smem] + [vmem] * len(terms),
        out_specs=[vmem, vmem],
        out_shape=[out, out],
        scratch_shapes=[pltpu.VMEM((SEQS * rank, 2 * rank), jnp.float32)],
        compiler_params=pltpu.CompilerParams(vmem_limit_bytes=VMEM // 4),
        name="product",
    )(edges, scale, *terms)


def shards(devices, activations, out_grads, proj_in, proj_out, seg_ids, queries):
    bits = devices.bit_length() - 1
    last = bits - 1
    rank = proj_in.shape[1]
    tokens = activations.shape[0]
    own = tokens // devices
    me = lax.axis_index("tp")

    def swap(value, bit):
        return lax.ppermute(value, "tp", [(i, i ^ (1 << bit)) for i in range(devices)])

    edges = jnp.sum(
        (seg_ids[None, :] < jnp.arange(SEQS + 1, dtype=jnp.int32)[:, None]).astype(jnp.int32), axis=1
    )
    scale = 1.0 / (edges[1:] - edges[:-1]).astype(jnp.float32)

    shares = tuple(own * share // UNITS for share in CHUNKS)
    chunks = len(shares)
    halves = project(bits, shares, activations, out_grads, proj_in.T, proj_out.T)
    sends, keeps = list(halves[0::2]), list(halves[1::2])
    on_both = [k >= chunks - BOTH_SIDES for k in range(chunks)]
    moves = sorted(
        ((k, b) for k in range(chunks) for b in range(bits)),
        key=lambda move: (0 if move[1] == 0 else move[0] + move[1], move[1], move[0]),
    )
    latest = None
    for k, b in moves:
        send, keep = sends[k], keeps[k]
        both = b == last and on_both[k]
        received = swap(jnp.concatenate([send, keep], axis=0) if both else send, b)
        if latest is not None:
            received, _ = lax.optimization_barrier((received, latest))
        if both:
            keeps[k] = latest = jnp.concatenate([keep, send], axis=0) + received
        elif b == last:
            keeps[k] = latest = keep + received
        else:
            half = keep.shape[0] // 2
            sends[k] = latest = keep[half:] + received[half:]
            keeps[k] = keep[:half] + received[:half]
    pieces = [(sum(shares[:k]), shares[k], 2 if on_both[k] else 1) for k in range(chunks)]
    early = [(keeps[k], pieces[k]) for k in range(chunks) if not on_both[k]]
    late = [(keeps[k], pieces[k]) for k in range(chunks) if on_both[k]]

    def group_product(group):
        return product(tuple(p for _, p in group), bits, own, edges, scale, [t for t, _ in group])

    send, keep = group_product(early)
    grads = keep + swap(send, 0)
    grads = grads + swap(grads, last)
    send, keep = group_product(late)
    grads = grads + keep + swap(send, 0)
    for b in range(1, last):
        grads = grads + swap(grads, b)
    pair = jnp.concatenate([grads, swap(grads, 0)], axis=0).reshape(SEQS, rank * rank)
    scores = jnp.dot(
        pair, queries.T, precision=lax.Precision.HIGHEST, preferred_element_type=jnp.float32
    )
    turned = jnp.concatenate([scores[SEQS // 2 :], scores[: SEQS // 2]], axis=0)
    return jnp.where((me & 1) == 0, scores, turned)


def solution(mesh):
    placed = (P("grp", "tp"), P("grp", "tp"), P("tp", None), P("tp", None), P("grp"), P("tp", None))
    return jax.shard_map(
        functools.partial(shards, mesh.shape["tp"]),
        mesh=mesh,
        in_specs=placed,
        out_specs=P("grp", "tp"),
        check_vma=False,
    )
```

```python
import functools

import jax
import jax.numpy as jnp
from jax import lax
from jax.experimental import pallas as pl
from jax.experimental.pallas import tpu as pltpu
from jax.sharding import PartitionSpec as P

SEQS = 8
UNITS = 16
CHUNKS = (4, 4, 4, 4)
BOTH_SIDES = 0
RING = 4
COST = 1
EARLY = 0
PAIR = 2
JOIN = 1
CROSSED = (1, 3)
CUT = 4
VMEM = 48 * 1024 * 1024
ROWS_BY_ROWS = (((1,), (1,)), ((), ()))


def project_kernel(bits, own, first, shares, a_hbm, g_hbm, pi_hbm, po_hbm, *refs):
    outs, (pi_ref, po_ref, a_buf, g_buf, sems) = refs[:-5], refs[-5:]
    ring, size = a_buf.shape[0], a_buf.shape[1]
    blocks = 1 << bits
    half = blocks // 2
    me_rev = reversed_index(bits)

    def copies(step):
        slot = lax.rem(step, ring)
        start = pl.multiple_of((step ^ me_rev) * own + first, 16)
        return (
            pltpu.make_async_copy(a_hbm.at[pl.ds(start, size), :], a_buf.at[slot], sems.at[slot, 0]),
            pltpu.make_async_copy(g_hbm.at[pl.ds(start, size), :], g_buf.at[slot], sems.at[slot, 1]),
        )

    weights = (
        pltpu.make_async_copy(pi_hbm, pi_ref, sems.at[ring, 0]),
        pltpu.make_async_copy(po_hbm, po_ref, sems.at[ring, 1]),
    )
    for copy in weights:
        copy.start()
    for step in range(ring - 1):
        for copy in copies(jnp.int32(step)):
            copy.start()
    for copy in weights:
        copy.wait()

    def body(step, carry):
        @pl.when(step + ring - 1 < blocks)
        def _():
            for copy in copies(step + ring - 1):
                copy.start()

        for copy in copies(step):
            copy.wait()
        slot = lax.rem(step, ring)
        side_x = lax.dot_general(a_buf[slot], pi_ref[...], ROWS_BY_ROWS, preferred_element_type=jnp.float32)
        side_g = lax.dot_general(g_buf[slot], po_ref[...], ROWS_BY_ROWS, preferred_element_type=jnp.float32)
        both = jnp.concatenate([side_x, side_g], axis=1)
        place = step & (half - 1)

        def store(out_refs):
            row = 0
            for share, out_ref in zip(shares, out_refs, strict=True):
                start = pl.multiple_of(place * share, 8)
                out_ref[pl.ds(start, share), :] = both[row : row + share]
                row += share

        @pl.when(step < half)
        def _():
            store(outs[1::2])

        @pl.when(step >= half)
        def _():
            store(outs[0::2])

        return carry

    lax.fori_loop(0, blocks, body, 0)


def reversed_index(bits):
    me = lax.axis_index("tp").astype(jnp.int32)
    flipped = jnp.int32(0)
    for b in range(bits):
        flipped = flipped | (((me >> b) & 1) << (bits - 1 - b))
    return flipped


def project(bits, first, shares, activations, out_grads, proj_in, proj_out):
    tokens, width = activations.shape
    hidden = out_grads.shape[1]
    rank = proj_in.shape[0]
    size = sum(shares)
    ring = min(RING, 1 << bits)
    outs = [
        jax.ShapeDtypeStruct(((1 << bits) // 2 * share, 2 * rank), jnp.float32)
        for share in shares
        for _ in range(2)
    ]
    vmem = pl.BlockSpec(memory_space=pltpu.VMEM)
    return pl.pallas_call(
        functools.partial(project_kernel, bits, tokens >> bits, first, shares),
        in_specs=[pl.BlockSpec(memory_space=pl.ANY)] * 4,
        out_specs=[vmem] * len(outs),
        out_shape=outs,
        scratch_shapes=[
            pltpu.VMEM(proj_in.shape, proj_in.dtype),
            pltpu.VMEM(proj_out.shape, proj_out.dtype),
            pltpu.VMEM((ring, size, width), activations.dtype),
            pltpu.VMEM((ring, size, hidden), out_grads.dtype),
            pltpu.SemaphoreType.DMA((ring + 1, 2)),
        ],
        compiler_params=pltpu.CompilerParams(vmem_limit_bytes=VMEM),
        cost_estimate=pl.CostEstimate(flops=COST, bytes_accessed=COST, transcendentals=0),
        name="project",
    )(activations, out_grads, proj_in, proj_out)


def product_kernel(pieces, bits, own, edge_ref, scale_ref, *refs):
    term_refs = refs[: len(pieces)]
    send_ref, keep_ref, held_ref = refs[len(pieces) :]
    terms = jnp.concatenate([ref[...] for ref in term_refs], axis=0)
    total_rows = terms.shape[0]
    rank = terms.shape[1] // 2
    me = reversed_index(bits)
    lane = lax.broadcasted_iota(jnp.int32, (1, total_rows), 1)
    token = lane
    offset = 0
    for first, rows, count in pieces:
        for part in range(count):
            start = (me ^ part) * own + first
            token = jnp.where(lane >= offset, lane + (start - offset), token)
            offset += rows
    proj_x = terms[:, :rank]
    x_hi = proj_x.astype(jnp.bfloat16)
    x_lo = (proj_x - x_hi.astype(jnp.float32)).astype(jnp.bfloat16)
    x_both = jnp.concatenate([x_hi, x_lo], axis=1)
    g_rows = terms.T[rank:, :]
    half = rank // 2
    side = me >> (bits - 1)
    group = SEQS // 2
    places = [place ^ (side * group) for place in range(SEQS)]
    high_parts, low_parts = [], []
    for s in places:
        inside = (token >= edge_ref[s]) & (token < edge_ref[s + 1])
        masked = jnp.where(inside, g_rows, 0.0)
        g_hi = masked.astype(jnp.bfloat16)
        high_parts.append(g_hi)
        low_parts.append((masked - g_hi.astype(jnp.float32)).astype(jnp.bfloat16))
    g_both = jnp.concatenate(high_parts + low_parts, axis=0)
    quad = jnp.dot(g_both, x_both, preferred_element_type=jnp.float32)
    upper, lower = quad[: SEQS * rank], quad[SEQS * rank :]
    total = upper[:, :rank] + (upper[:, rank:] + lower[:, :rank] + lower[:, rank:])
    for place, s in enumerate(places):
        rows = slice(place * rank, (place + 1) * rank)
        held_ref[rows, :rank] = total[rows] * scale_ref[s]
    even = held_ref[pl.ds(0, SEQS * half, stride=2), :]
    odd = held_ref[pl.ds(1, SEQS * half, stride=2), :]
    packed = jnp.concatenate([even[:, :rank], odd[:, :rank]], axis=1)
    keep_ref[...] = packed[: group * half]
    send_ref[...] = packed[group * half :]


def product(pieces, bits, own, edges, scale, terms):
    rank = terms[0].shape[1] // 2
    out = jax.ShapeDtypeStruct((SEQS // 2 * rank // 2, 2 * rank), jnp.float32)
    vmem = pl.BlockSpec(memory_space=pltpu.VMEM)
    smem = pl.BlockSpec(memory_space=pltpu.SMEM)
    return pl.pallas_call(
        functools.partial(product_kernel, pieces, bits, own),
        in_specs=[smem, smem] + [vmem] * len(terms),
        out_specs=[vmem, vmem],
        out_shape=[out, out],
        scratch_shapes=[pltpu.VMEM((SEQS * rank, 2 * rank), jnp.float32)],
        compiler_params=pltpu.CompilerParams(vmem_limit_bytes=VMEM // 4),
        name="product",
    )(edges, scale, *terms)


def shards(devices, activations, out_grads, proj_in, proj_out, seg_ids, queries):
    bits = devices.bit_length() - 1
    last = bits - 1
    rank = proj_in.shape[1]
    tokens = activations.shape[0]
    own = tokens // devices
    me = lax.axis_index("tp")

    def swap(value, bit):
        return lax.ppermute(value, "tp", [(i, i ^ (1 << bit)) for i in range(devices)])

    edges = jnp.sum(
        (seg_ids[None, :] < jnp.arange(SEQS + 1, dtype=jnp.int32)[:, None]).astype(jnp.int32), axis=1
    )
    scale = 1.0 / (edges[1:] - edges[:-1]).astype(jnp.float32)

    shares = tuple(own * share // UNITS for share in CHUNKS)
    chunks = len(shares)
    on_both = [k >= chunks - BOTH_SIDES for k in range(chunks)]
    weights = (proj_in.T, proj_out.T)
    halves = list(project(bits, 0, shares[:CUT], activations, out_grads, *weights))
    sends, keeps = halves[0::2], halves[1::2]

    def route(k):
        return [0, 2, 1, *range(3, bits)] if k in CROSSED else list(range(bits))

    def turn(k, stage):
        if stage == 0:
            return 0.0 if k < CUT else 0.5
        return 0.4 if stage == 1 and k < EARLY else float(k // PAIR + stage)

    def split(value, left, b):
        shape = (1 << left.index(b), 2, -1, value.shape[1])
        parts = value.reshape(shape)
        return parts[:, 1].reshape(-1, value.shape[1]), parts[:, 0].reshape(-1, value.shape[1])

    moves = sorted(
        ((k, stage) for k in range(chunks) for stage in range(bits)),
        key=lambda move: (turn(*move), move[1], move[0]),
    )
    remaining = [list(range(1, bits)) for _ in range(chunks)]
    latest = None
    for k, stage in moves:
        b = route(k)[stage]
        if len(sends) < chunks and stage == 1:
            weights, _ = lax.optimization_barrier((weights, sends))
            halves = list(project(bits, sum(shares[:CUT]), shares[CUT:], activations, out_grads, *weights))
            sends, keeps = sends + halves[0::2], keeps + halves[1::2]
        send, keep = sends[k], keeps[k]
        if b == last and not BOTH_SIDES:
            joined = [j for j in range(chunks) if j // JOIN == k // JOIN]
            if k == joined[-1]:
                send = jnp.concatenate([sends[j] for j in joined], axis=0)
                received, _ = lax.optimization_barrier((swap(send, b), latest))
                row = 0
                for j in joined:
                    keeps[j] = latest = keeps[j] + received[row : row + sends[j].shape[0]]
                    row += sends[j].shape[0]
            continue
        both = b == last and on_both[k]
        received = swap(jnp.concatenate([send, keep], axis=0) if both else send, b)
        if latest is not None:
            received, _ = lax.optimization_barrier((received, latest))
        if both:
            keeps[k] = latest = jnp.concatenate([keep, send], axis=0) + received
        elif b == last:
            keeps[k] = latest = keep + received
        else:
            following = route(k)[stage + 1]
            old, new = split(keep, remaining[k], following), split(received, remaining[k], following)
            remaining[k].remove(following)
            sends[k] = latest = old[0] + new[0]
            keeps[k] = old[1] + new[1]
    pieces = [(sum(shares[:k]), shares[k], 2 if on_both[k] else 1) for k in range(chunks)]
    early = [(keeps[k], pieces[k]) for k in range(chunks) if not on_both[k]]
    late = [(keeps[k], pieces[k]) for k in range(chunks) if on_both[k]]

    def group_product(group):
        return product(tuple(p for _, p in group), bits, own, edges, scale, [t for t, _ in group])

    send, keep = group_product(early or late)
    grads = keep + swap(send, 0)
    hops = range(1, last if late else bits)
    if early and late:
        grads = grads + swap(grads, last)
        send, keep = group_product(late)
        grads = grads + keep + swap(send, 0)
    for b in hops:
        grads = grads + swap(grads, b)
    other = swap(grads, 0)
    even = (me & 1) == 0
    pair = jnp.concatenate([jnp.where(even, grads, other), jnp.where(even, other, grads)], axis=0)
    return jnp.dot(
        pair.reshape(SEQS, rank * rank), queries.T, precision=lax.Precision.HIGHEST, preferred_element_type=jnp.float32
    )


def solution(mesh):
    placed = (P("grp", "tp"), P("grp", "tp"), P("tp", None), P("tp", None), P("grp"), P("tp", None))
    return jax.shard_map(
        functools.partial(shards, mesh.shape["tp"]),
        mesh=mesh,
        in_specs=placed,
        out_specs=P("grp", "tp"),
        check_vma=False,
    )
```

```python
import functools

import jax
import jax.numpy as jnp
from jax import lax
from jax.experimental import pallas as pl
from jax.experimental.pallas import tpu as pltpu
from jax.sharding import PartitionSpec as P

SEQS = 8
UNITS = 16
CHUNKS = (4, 4, 4, 4)
BOTH_SIDES = 0
RING = 4
COST = 1
EARLY = 0
PAIR = 2
JOIN = 1
CROSSED = (1, 3)
CUT = 4
VMEM = 48 * 1024 * 1024
ROWS_BY_ROWS = (((1,), (1,)), ((), ()))


def project_kernel(bits, own, first, shares, a_hbm, g_hbm, w_hbm, *refs):
    outs, (w_ref, a_buf, g_buf, sems) = refs[:-4], refs[-4:]
    width = a_buf.shape[2]
    ring, size = a_buf.shape[0], a_buf.shape[1]
    blocks = 1 << bits
    half = blocks // 2
    me_rev = reversed_index(bits)

    def copies(step):
        slot = lax.rem(step, ring)
        start = pl.multiple_of((step ^ me_rev) * own + first, 16)
        return (
            pltpu.make_async_copy(a_hbm.at[pl.ds(start, size), :], a_buf.at[slot], sems.at[slot, 0]),
            pltpu.make_async_copy(g_hbm.at[pl.ds(start, size), :], g_buf.at[slot], sems.at[slot, 1]),
        )

    weights = pltpu.make_async_copy(w_hbm, w_ref, sems.at[ring, 0])
    weights.start()
    for step in range(ring - 1):
        for copy in copies(jnp.int32(step)):
            copy.start()
    weights.wait()

    def body(step, carry):
        @pl.when(step + ring - 1 < blocks)
        def _():
            for copy in copies(step + ring - 1):
                copy.start()

        for copy in copies(step):
            copy.wait()
        slot = lax.rem(step, ring)
        side_x = lax.dot_general(a_buf[slot], w_ref[:, :width], ROWS_BY_ROWS, preferred_element_type=jnp.float32)
        side_g = lax.dot_general(g_buf[slot], w_ref[:, width:], ROWS_BY_ROWS, preferred_element_type=jnp.float32)
        both = jnp.concatenate([side_x, side_g], axis=1)
        place = step & (half - 1)

        def store(out_refs):
            row = 0
            for share, out_ref in zip(shares, out_refs, strict=True):
                start = pl.multiple_of(place * share, 8)
                out_ref[pl.ds(start, share), :] = both[row : row + share]
                row += share

        @pl.when(step < half)
        def _():
            store(outs[1::2])

        @pl.when(step >= half)
        def _():
            store(outs[0::2])

        return carry

    lax.fori_loop(0, blocks, body, 0)


def reversed_index(bits):
    me = lax.axis_index("tp").astype(jnp.int32)
    flipped = jnp.int32(0)
    for b in range(bits):
        flipped = flipped | (((me >> b) & 1) << (bits - 1 - b))
    return flipped


def project(bits, first, shares, activations, out_grads, weights):
    tokens, width = activations.shape
    hidden = out_grads.shape[1]
    rank = weights.shape[0]
    size = sum(shares)
    ring = min(RING, 1 << bits)
    outs = [
        jax.ShapeDtypeStruct(((1 << bits) // 2 * share, 2 * rank), jnp.float32)
        for share in shares
        for _ in range(2)
    ]
    vmem = pl.BlockSpec(memory_space=pltpu.VMEM)
    return pl.pallas_call(
        functools.partial(project_kernel, bits, tokens >> bits, first, shares),
        in_specs=[pl.BlockSpec(memory_space=pl.ANY)] * 3,
        out_specs=[vmem] * len(outs),
        out_shape=outs,
        scratch_shapes=[
            pltpu.VMEM(weights.shape, weights.dtype),
            pltpu.VMEM((ring, size, width), activations.dtype),
            pltpu.VMEM((ring, size, hidden), out_grads.dtype),
            pltpu.SemaphoreType.DMA((ring + 1, 2)),
        ],
        compiler_params=pltpu.CompilerParams(vmem_limit_bytes=VMEM),
        cost_estimate=pl.CostEstimate(flops=COST, bytes_accessed=COST, transcendentals=0),
        name="project",
    )(activations, out_grads, weights)


def product_kernel(pieces, bits, own, edge_ref, scale_ref, *refs):
    term_refs = refs[: len(pieces)]
    send_ref, keep_ref, held_ref = refs[len(pieces) :]
    terms = jnp.concatenate([ref[...] for ref in term_refs], axis=0)
    total_rows = terms.shape[0]
    rank = terms.shape[1] // 2
    me = reversed_index(bits)
    lane = lax.broadcasted_iota(jnp.int32, (1, total_rows), 1)
    token = lane
    offset = 0
    for first, rows, count in pieces:
        for part in range(count):
            start = (me ^ part) * own + first
            token = jnp.where(lane >= offset, lane + (start - offset), token)
            offset += rows
    proj_x = terms[:, :rank]
    x_hi = proj_x.astype(jnp.bfloat16)
    x_lo = (proj_x - x_hi.astype(jnp.float32)).astype(jnp.bfloat16)
    x_both = jnp.concatenate([x_hi, x_lo], axis=1)
    g_rows = terms.T[rank:, :]
    half = rank // 2
    side = me >> (bits - 1)
    group = SEQS // 2
    places = [place ^ (side * group) for place in range(SEQS)]
    high_parts, low_parts = [], []
    for s in places:
        inside = (token >= edge_ref[s]) & (token < edge_ref[s + 1])
        masked = jnp.where(inside, g_rows, 0.0)
        g_hi = masked.astype(jnp.bfloat16)
        high_parts.append(g_hi)
        low_parts.append((masked - g_hi.astype(jnp.float32)).astype(jnp.bfloat16))
    g_both = jnp.concatenate(high_parts + low_parts, axis=0)
    quad = jnp.dot(g_both, x_both, preferred_element_type=jnp.float32)
    upper, lower = quad[: SEQS * rank], quad[SEQS * rank :]
    total = upper[:, :rank] + (upper[:, rank:] + lower[:, :rank] + lower[:, rank:])
    for place, s in enumerate(places):
        rows = slice(place * rank, (place + 1) * rank)
        held_ref[rows, :rank] = total[rows] * scale_ref[s]
    even = held_ref[pl.ds(0, SEQS * half, stride=2), :]
    odd = held_ref[pl.ds(1, SEQS * half, stride=2), :]
    packed = jnp.concatenate([even[:, :rank], odd[:, :rank]], axis=1)
    keep_ref[...] = packed[: group * half]
    send_ref[...] = packed[group * half :]


def product(pieces, bits, own, edges, scale, terms):
    rank = terms[0].shape[1] // 2
    out = jax.ShapeDtypeStruct((SEQS // 2 * rank // 2, 2 * rank), jnp.float32)
    vmem = pl.BlockSpec(memory_space=pltpu.VMEM)
    smem = pl.BlockSpec(memory_space=pltpu.SMEM)
    return pl.pallas_call(
        functools.partial(product_kernel, pieces, bits, own),
        in_specs=[smem, smem] + [vmem] * len(terms),
        out_specs=[vmem, vmem],
        out_shape=[out, out],
        scratch_shapes=[pltpu.VMEM((SEQS * rank, 2 * rank), jnp.float32)],
        compiler_params=pltpu.CompilerParams(vmem_limit_bytes=VMEM // 4),
        name="product",
    )(edges, scale, *terms)


def shards(devices, activations, out_grads, proj_in, proj_out, seg_ids, queries):
    bits = devices.bit_length() - 1
    last = bits - 1
    rank = proj_in.shape[1]
    tokens = activations.shape[0]
    own = tokens // devices
    me = lax.axis_index("tp")

    def swap(value, bit):
        return lax.ppermute(value, "tp", [(i, i ^ (1 << bit)) for i in range(devices)])

    edges = jnp.sum(
        (seg_ids[None, :] < jnp.arange(SEQS + 1, dtype=jnp.int32)[:, None]).astype(jnp.int32), axis=1
    )
    scale = 1.0 / (edges[1:] - edges[:-1]).astype(jnp.float32)

    shares = tuple(own * share // UNITS for share in CHUNKS)
    chunks = len(shares)
    on_both = [k >= chunks - BOTH_SIDES for k in range(chunks)]
    weights = jnp.concatenate([proj_in.T, proj_out.T], axis=1)
    halves = list(project(bits, 0, shares[:CUT], activations, out_grads, weights))
    sends, keeps = halves[0::2], halves[1::2]

    def route(k):
        return [0, 2, 1, *range(3, bits)] if k in CROSSED else list(range(bits))

    def turn(k, stage):
        if stage == 0:
            return 0.0 if k < CUT else 0.5
        return 0.4 if stage == 1 and k < EARLY else float(k // PAIR + stage)

    def split(value, left, b):
        shape = (1 << left.index(b), 2, -1, value.shape[1])
        parts = value.reshape(shape)
        return parts[:, 1].reshape(-1, value.shape[1]), parts[:, 0].reshape(-1, value.shape[1])

    moves = sorted(
        ((k, stage) for k in range(chunks) for stage in range(bits)),
        key=lambda move: (turn(*move), move[1], move[0]),
    )
    remaining = [list(range(1, bits)) for _ in range(chunks)]
    latest = None
    for k, stage in moves:
        b = route(k)[stage]
        if len(sends) < chunks and stage == 1:
            weights, _ = lax.optimization_barrier((weights, sends))
            halves = list(project(bits, sum(shares[:CUT]), shares[CUT:], activations, out_grads, weights))
            sends, keeps = sends + halves[0::2], keeps + halves[1::2]
        send, keep = sends[k], keeps[k]
        if b == last and not BOTH_SIDES:
            joined = [j for j in range(chunks) if j // JOIN == k // JOIN]
            if k == joined[-1]:
                send = jnp.concatenate([sends[j] for j in joined], axis=0)
                received, _ = lax.optimization_barrier((swap(send, b), latest))
                row = 0
                for j in joined:
                    keeps[j] = latest = keeps[j] + received[row : row + sends[j].shape[0]]
                    row += sends[j].shape[0]
            continue
        both = b == last and on_both[k]
        received = swap(jnp.concatenate([send, keep], axis=0) if both else send, b)
        if latest is not None:
            received, _ = lax.optimization_barrier((received, latest))
        if both:
            keeps[k] = latest = jnp.concatenate([keep, send], axis=0) + received
        elif b == last:
            keeps[k] = latest = keep + received
        else:
            following = route(k)[stage + 1]
            old, new = split(keep, remaining[k], following), split(received, remaining[k], following)
            remaining[k].remove(following)
            sends[k] = latest = old[0] + new[0]
            keeps[k] = old[1] + new[1]
    pieces = [(sum(shares[:k]), shares[k], 2 if on_both[k] else 1) for k in range(chunks)]
    early = [(keeps[k], pieces[k]) for k in range(chunks) if not on_both[k]]
    late = [(keeps[k], pieces[k]) for k in range(chunks) if on_both[k]]

    def group_product(group):
        return product(tuple(p for _, p in group), bits, own, edges, scale, [t for t, _ in group])

    send, keep = group_product(early or late)
    grads = keep + swap(send, 0)
    hops = range(1, last if late else bits)
    if early and late:
        grads = grads + swap(grads, last)
        send, keep = group_product(late)
        grads = grads + keep + swap(send, 0)
    for b in hops:
        grads = grads + swap(grads, b)
    other = swap(grads, 0)
    even = (me & 1) == 0
    pair = jnp.concatenate([jnp.where(even, grads, other), jnp.where(even, other, grads)], axis=0)
    return jnp.dot(
        pair.reshape(SEQS, rank * rank), queries.T, precision=lax.Precision.HIGHEST, preferred_element_type=jnp.float32
    )


def solution(mesh):
    placed = (P("grp", "tp"), P("grp", "tp"), P("tp", None), P("tp", None), P("grp"), P("tp", None))
    return jax.shard_map(
        functools.partial(shards, mesh.shape["tp"]),
        mesh=mesh,
        in_specs=placed,
        out_specs=P("grp", "tp"),
        check_vma=False,
    )
```

```python
import functools

import jax
import jax.numpy as jnp
from jax import lax
from jax.experimental import pallas as pl
from jax.experimental.pallas import tpu as pltpu
from jax.sharding import PartitionSpec as P

SEQS = 8
UNITS = 16
CHUNKS = (4, 4, 4, 4)
BOTH_SIDES = 0
RING = 4
COST = 1
EARLY = 0
PAIR = 2
JOIN = 1
CROSSED = (1, 3)
CUT = 4
VMEM = 48 * 1024 * 1024
ROWS_BY_ROWS = (((1,), (1,)), ((), ()))


def project_kernel(bits, own, first, shares, a_hbm, g_hbm, w_hbm, *refs):
    outs, (w_ref, a_buf, g_buf, sems) = refs[:-4], refs[-4:]
    width = a_buf.shape[2]
    ring, size = a_buf.shape[0], a_buf.shape[1]
    blocks = 1 << bits
    half = blocks // 2
    me_rev = reversed_index(bits)

    def copies(step):
        slot = lax.rem(step, ring)
        start = pl.multiple_of((step ^ me_rev) * own + first, 16)
        return (
            pltpu.make_async_copy(a_hbm.at[pl.ds(start, size), :], a_buf.at[slot], sems.at[slot, 0]),
            pltpu.make_async_copy(g_hbm.at[pl.ds(start, size), :], g_buf.at[slot], sems.at[slot, 1]),
        )

    weights = pltpu.make_async_copy(w_hbm, w_ref, sems.at[ring, 0])
    weights.start()
    for step in range(ring - 1):
        for copy in copies(jnp.int32(step)):
            copy.start()
    weights.wait()

    def body(step, carry):
        @pl.when(step + ring - 1 < blocks)
        def _():
            for copy in copies(step + ring - 1):
                copy.start()

        for copy in copies(step):
            copy.wait()
        slot = lax.rem(step, ring)
        side_x = lax.dot_general(a_buf[slot], w_ref[:, :width], ROWS_BY_ROWS, preferred_element_type=jnp.float32)
        side_g = lax.dot_general(g_buf[slot], w_ref[:, width:], ROWS_BY_ROWS, preferred_element_type=jnp.float32)
        both = jnp.concatenate([side_x, side_g], axis=1)
        place = step & (half - 1)

        def store(out_refs):
            row = 0
            for share, out_ref in zip(shares, out_refs, strict=True):
                start = pl.multiple_of(place * share, 8)
                out_ref[pl.ds(start, share), :] = both[row : row + share]
                row += share

        @pl.when(step < half)
        def _():
            store(outs[1::2])

        @pl.when(step >= half)
        def _():
            store(outs[0::2])

        return carry

    lax.fori_loop(0, blocks, body, 0)


def reversed_index(bits):
    me = lax.axis_index("tp").astype(jnp.int32)
    flipped = jnp.int32(0)
    for b in range(bits):
        flipped = flipped | (((me >> b) & 1) << (bits - 1 - b))
    return flipped


def project(bits, first, shares, activations, out_grads, weights):
    tokens, width = activations.shape
    hidden = out_grads.shape[1]
    rank = weights.shape[0]
    size = sum(shares)
    ring = min(RING, 1 << bits)
    outs = [
        jax.ShapeDtypeStruct(((1 << bits) // 2 * share, 2 * rank), jnp.float32)
        for share in shares
        for _ in range(2)
    ]
    vmem = pl.BlockSpec(memory_space=pltpu.VMEM)
    return pl.pallas_call(
        functools.partial(project_kernel, bits, tokens >> bits, first, shares),
        in_specs=[pl.BlockSpec(memory_space=pl.ANY)] * 3,
        out_specs=[vmem] * len(outs),
        out_shape=outs,
        scratch_shapes=[
            pltpu.VMEM(weights.shape, weights.dtype),
            pltpu.VMEM((ring, size, width), activations.dtype),
            pltpu.VMEM((ring, size, hidden), out_grads.dtype),
            pltpu.SemaphoreType.DMA((ring + 1, 2)),
        ],
        compiler_params=pltpu.CompilerParams(vmem_limit_bytes=VMEM),
        cost_estimate=pl.CostEstimate(flops=COST, bytes_accessed=COST, transcendentals=0),
        name="project",
    )(activations, out_grads, weights)


def product_kernel(pieces, bits, own, edge_ref, scale_ref, *refs):
    term_refs = refs[: len(pieces)]
    send_ref, keep_ref, held_ref = refs[len(pieces) :]
    terms = jnp.concatenate([ref[...] for ref in term_refs], axis=0)
    total_rows = terms.shape[0]
    rank = terms.shape[1] // 2
    me = reversed_index(bits)
    lane = lax.broadcasted_iota(jnp.int32, (1, total_rows), 1)
    token = lane
    offset = 0
    for first, rows, count in pieces:
        for part in range(count):
            start = (me ^ part) * own + first
            token = jnp.where(lane >= offset, lane + (start - offset), token)
            offset += rows
    proj_x = terms[:, :rank]
    x_hi = proj_x.astype(jnp.bfloat16)
    x_lo = (proj_x - x_hi.astype(jnp.float32)).astype(jnp.bfloat16)
    x_both = jnp.concatenate([x_hi, x_lo], axis=1)
    g_rows = terms.T[rank:, :]
    half = rank // 2
    side = me >> (bits - 1)
    group = SEQS // 2
    places = [place ^ (side * group) for place in range(SEQS)]
    high_parts, low_parts = [], []
    for s in places:
        inside = (token >= edge_ref[s]) & (token < edge_ref[s + 1])
        masked = jnp.where(inside, g_rows, 0.0)
        g_hi = masked.astype(jnp.bfloat16)
        high_parts.append(g_hi)
        low_parts.append((masked - g_hi.astype(jnp.float32)).astype(jnp.bfloat16))
    g_both = jnp.concatenate(high_parts + low_parts, axis=0)
    quad = jnp.dot(g_both, x_both, preferred_element_type=jnp.float32)
    upper, lower = quad[: SEQS * rank], quad[SEQS * rank :]
    total = upper[:, :rank] + (upper[:, rank:] + lower[:, :rank] + lower[:, rank:])
    for place, s in enumerate(places):
        rows = slice(place * rank, (place + 1) * rank)
        held_ref[rows, :rank] = total[rows] * scale_ref[s]
    even = held_ref[pl.ds(0, SEQS * half, stride=2), :]
    odd = held_ref[pl.ds(1, SEQS * half, stride=2), :]
    packed = jnp.concatenate([even[:, :rank], odd[:, :rank]], axis=1)
    keep_ref[...] = packed[: group * half]
    send_ref[...] = packed[group * half :]


def product(pieces, bits, own, edges, scale, terms):
    rank = terms[0].shape[1] // 2
    out = jax.ShapeDtypeStruct((SEQS // 2 * rank // 2, 2 * rank), jnp.float32)
    vmem = pl.BlockSpec(memory_space=pltpu.VMEM)
    smem = pl.BlockSpec(memory_space=pltpu.SMEM)
    return pl.pallas_call(
        functools.partial(product_kernel, pieces, bits, own),
        in_specs=[smem, smem] + [vmem] * len(terms),
        out_specs=[vmem, vmem],
        out_shape=[out, out],
        scratch_shapes=[pltpu.VMEM((SEQS * rank, 2 * rank), jnp.float32)],
        compiler_params=pltpu.CompilerParams(vmem_limit_bytes=VMEM // 4),
        name="product",
    )(edges, scale, *terms)


def shards(devices, activations, out_grads, proj_in, proj_out, seg_ids, queries):
    bits = devices.bit_length() - 1
    last = bits - 1
    rank = proj_in.shape[1]
    tokens = activations.shape[0]
    own = tokens // devices
    me = lax.axis_index("tp")

    def exchange(value, mask):
        return lax.ppermute(value, "tp", [(i, i ^ mask) for i in range(devices)])

    def swap(value, bit):
        return exchange(value, 1 << bit)

    edges = jnp.sum(
        (seg_ids[None, :] < jnp.arange(SEQS + 1, dtype=jnp.int32)[:, None]).astype(jnp.int32), axis=1
    )
    scale = 1.0 / (edges[1:] - edges[:-1]).astype(jnp.float32)

    shares = tuple(own * share // UNITS for share in CHUNKS)
    chunks = len(shares)
    on_both = [k >= chunks - BOTH_SIDES for k in range(chunks)]
    weights = jnp.concatenate([proj_in.T, proj_out.T], axis=1)
    halves = list(project(bits, 0, shares[:CUT], activations, out_grads, weights))
    sends, keeps = halves[0::2], halves[1::2]

    def route(k):
        return [0, 2, 1, *range(3, bits)] if k in CROSSED else list(range(bits))

    def turn(k, stage):
        if stage == 0:
            return 0.0 if k < CUT else 0.5
        return 0.4 if stage == 1 and k < EARLY else float(k // PAIR + stage)

    def split(value, left, b):
        shape = (1 << left.index(b), 2, -1, value.shape[1])
        parts = value.reshape(shape)
        return parts[:, 1].reshape(-1, value.shape[1]), parts[:, 0].reshape(-1, value.shape[1])

    moves = sorted(
        ((k, stage) for k in range(chunks) for stage in range(bits)),
        key=lambda move: (turn(*move), move[1], move[0]),
    )
    remaining = [list(range(1, bits)) for _ in range(chunks)]
    latest = None
    for k, stage in moves:
        b = route(k)[stage]
        if len(sends) < chunks and stage == 1:
            weights, _ = lax.optimization_barrier((weights, sends))
            halves = list(project(bits, sum(shares[:CUT]), shares[CUT:], activations, out_grads, weights))
            sends, keeps = sends + halves[0::2], keeps + halves[1::2]
        send, keep = sends[k], keeps[k]
        if b == last and not BOTH_SIDES:
            joined = [j for j in range(chunks) if j // JOIN == k // JOIN]
            if k == joined[-1]:
                send = jnp.concatenate([sends[j] for j in joined], axis=0)
                received, _ = lax.optimization_barrier((swap(send, b), latest))
                row = 0
                for j in joined:
                    keeps[j] = latest = keeps[j] + received[row : row + sends[j].shape[0]]
                    row += sends[j].shape[0]
            continue
        both = b == last and on_both[k]
        received = swap(jnp.concatenate([send, keep], axis=0) if both else send, b)
        if latest is not None:
            received, _ = lax.optimization_barrier((received, latest))
        if both:
            keeps[k] = latest = jnp.concatenate([keep, send], axis=0) + received
        elif b == last:
            keeps[k] = latest = keep + received
        else:
            following = route(k)[stage + 1]
            old, new = split(keep, remaining[k], following), split(received, remaining[k], following)
            remaining[k].remove(following)
            sends[k] = latest = old[0] + new[0]
            keeps[k] = old[1] + new[1]
    pieces = [(sum(shares[:k]), shares[k], 2 if on_both[k] else 1) for k in range(chunks)]
    early = [(keeps[k], pieces[k]) for k in range(chunks) if not on_both[k]]
    late = [(keeps[k], pieces[k]) for k in range(chunks) if on_both[k]]

    def group_product(group):
        return product(tuple(p for _, p in group), bits, own, edges, scale, [t for t, _ in group])

    send, keep = group_product(early or late)
    grads = keep + swap(send, 0)
    hops = range(1, last if late else bits)
    if early and late:
        grads = grads + swap(grads, last)
        send, keep = group_product(late)
        grads = grads + keep + swap(send, 0)
    grads = (grads + exchange(grads, 6)) + (exchange(grads, 2) + exchange(grads, 4))
    for b in hops:
        if b > 2:
            grads = grads + swap(grads, b)
    other = swap(grads, 0)
    even = (me & 1) == 0
    pair = jnp.concatenate([jnp.where(even, grads, other), jnp.where(even, other, grads)], axis=0)
    return jnp.dot(
        pair.reshape(SEQS, rank * rank), queries.T, precision=lax.Precision.HIGHEST, preferred_element_type=jnp.float32
    )


def solution(mesh):
    placed = (P("grp", "tp"), P("grp", "tp"), P("tp", None), P("tp", None), P("grp"), P("tp", None))
    return jax.shard_map(
        functools.partial(shards, mesh.shape["tp"]),
        mesh=mesh,
        in_specs=placed,
        out_specs=P("grp", "tp"),
        check_vma=False,
    )
```

```python
import functools

import jax
import jax.numpy as jnp
from jax import lax
from jax.experimental import pallas as pl
from jax.experimental.pallas import tpu as pltpu
from jax.sharding import PartitionSpec as P

SEQS = 8
UNITS = 16
CHUNKS = (4, 4, 5, 3)
BOTH_SIDES = 0
RING = 4
COST = 1
EARLY = 0
PAIR = 2
JOIN = 1
CROSSED = (1, 3)
CUT = 4
VMEM = 48 * 1024 * 1024
ROWS_BY_ROWS = (((1,), (1,)), ((), ()))


def project_kernel(bits, own, first, shares, a_hbm, g_hbm, w_hbm, *refs):
    outs, (w_ref, a_buf, g_buf, sems) = refs[:-4], refs[-4:]
    width = a_buf.shape[2]
    ring, size = a_buf.shape[0], a_buf.shape[1]
    blocks = 1 << bits
    half = blocks // 2
    me_rev = reversed_index(bits)

    def copies(step):
        slot = lax.rem(step, ring)
        start = pl.multiple_of((step ^ me_rev) * own + first, 16)
        return (
            pltpu.make_async_copy(a_hbm.at[pl.ds(start, size), :], a_buf.at[slot], sems.at[slot, 0]),
            pltpu.make_async_copy(g_hbm.at[pl.ds(start, size), :], g_buf.at[slot], sems.at[slot, 1]),
        )

    weights = pltpu.make_async_copy(w_hbm, w_ref, sems.at[ring, 0])
    weights.start()
    for step in range(ring - 1):
        for copy in copies(jnp.int32(step)):
            copy.start()
    weights.wait()

    def body(step, carry):
        @pl.when(step + ring - 1 < blocks)
        def _():
            for copy in copies(step + ring - 1):
                copy.start()

        for copy in copies(step):
            copy.wait()
        slot = lax.rem(step, ring)
        side_x = lax.dot_general(a_buf[slot], w_ref[:, :width], ROWS_BY_ROWS, preferred_element_type=jnp.float32)
        side_g = lax.dot_general(g_buf[slot], w_ref[:, width:], ROWS_BY_ROWS, preferred_element_type=jnp.float32)
        both = jnp.concatenate([side_x, side_g], axis=1)
        place = step & (half - 1)

        def store(out_refs):
            row = 0
            for share, out_ref in zip(shares, out_refs, strict=True):
                start = pl.multiple_of(place * share, 8)
                out_ref[pl.ds(start, share), :] = both[row : row + share]
                row += share

        @pl.when(step < half)
        def _():
            store(outs[1::2])

        @pl.when(step >= half)
        def _():
            store(outs[0::2])

        return carry

    lax.fori_loop(0, blocks, body, 0)


def reversed_index(bits):
    me = lax.axis_index("tp").astype(jnp.int32)
    flipped = jnp.int32(0)
    for b in range(bits):
        flipped = flipped | (((me >> b) & 1) << (bits - 1 - b))
    return flipped


def project(bits, first, shares, activations, out_grads, weights):
    tokens, width = activations.shape
    hidden = out_grads.shape[1]
    rank = weights.shape[0]
    size = sum(shares)
    ring = min(RING, 1 << bits)
    outs = [
        jax.ShapeDtypeStruct(((1 << bits) // 2 * share, 2 * rank), jnp.float32)
        for share in shares
        for _ in range(2)
    ]
    vmem = pl.BlockSpec(memory_space=pltpu.VMEM)
    return pl.pallas_call(
        functools.partial(project_kernel, bits, tokens >> bits, first, shares),
        in_specs=[pl.BlockSpec(memory_space=pl.ANY)] * 3,
        out_specs=[vmem] * len(outs),
        out_shape=outs,
        scratch_shapes=[
            pltpu.VMEM(weights.shape, weights.dtype),
            pltpu.VMEM((ring, size, width), activations.dtype),
            pltpu.VMEM((ring, size, hidden), out_grads.dtype),
            pltpu.SemaphoreType.DMA((ring + 1, 2)),
        ],
        compiler_params=pltpu.CompilerParams(vmem_limit_bytes=VMEM),
        cost_estimate=pl.CostEstimate(flops=COST, bytes_accessed=COST, transcendentals=0),
        name="project",
    )(activations, out_grads, weights)


def product_kernel(pieces, bits, own, edge_ref, scale_ref, *refs):
    term_refs = refs[: len(pieces)]
    send_ref, keep_ref, held_ref = refs[len(pieces) :]
    terms = jnp.concatenate([ref[...] for ref in term_refs], axis=0)
    total_rows = terms.shape[0]
    rank = terms.shape[1] // 2
    me = reversed_index(bits)
    lane = lax.broadcasted_iota(jnp.int32, (1, total_rows), 1)
    token = lane
    offset = 0
    for first, rows, count in pieces:
        for part in range(count):
            start = (me ^ part) * own + first
            token = jnp.where(lane >= offset, lane + (start - offset), token)
            offset += rows
    proj_x = terms[:, :rank]
    x_hi = proj_x.astype(jnp.bfloat16)
    x_lo = (proj_x - x_hi.astype(jnp.float32)).astype(jnp.bfloat16)
    x_both = jnp.concatenate([x_hi, x_lo], axis=1)
    g_rows = terms.T[rank:, :]
    half = rank // 2
    side = me >> (bits - 1)
    group = SEQS // 2
    places = [place ^ (side * group) for place in range(SEQS)]
    high_parts, low_parts = [], []
    for s in places:
        inside = (token >= edge_ref[s]) & (token < edge_ref[s + 1])
        masked = jnp.where(inside, g_rows, 0.0)
        g_hi = masked.astype(jnp.bfloat16)
        high_parts.append(g_hi)
        low_parts.append((masked - g_hi.astype(jnp.float32)).astype(jnp.bfloat16))
    g_both = jnp.concatenate(high_parts + low_parts, axis=0)
    quad = jnp.dot(g_both, x_both, preferred_element_type=jnp.float32)
    upper, lower = quad[: SEQS * rank], quad[SEQS * rank :]
    total = upper[:, :rank] + (upper[:, rank:] + lower[:, :rank] + lower[:, rank:])
    for place, s in enumerate(places):
        rows = slice(place * rank, (place + 1) * rank)
        held_ref[rows, :rank] = total[rows] * scale_ref[s]
    even = held_ref[pl.ds(0, SEQS * half, stride=2), :]
    odd = held_ref[pl.ds(1, SEQS * half, stride=2), :]
    packed = jnp.concatenate([even[:, :rank], odd[:, :rank]], axis=1)
    keep_ref[...] = packed[: group * half]
    send_ref[...] = packed[group * half :]


def product(pieces, bits, own, edges, scale, terms):
    rank = terms[0].shape[1] // 2
    out = jax.ShapeDtypeStruct((SEQS // 2 * rank // 2, 2 * rank), jnp.float32)
    vmem = pl.BlockSpec(memory_space=pltpu.VMEM)
    smem = pl.BlockSpec(memory_space=pltpu.SMEM)
    return pl.pallas_call(
        functools.partial(product_kernel, pieces, bits, own),
        in_specs=[smem, smem] + [vmem] * len(terms),
        out_specs=[vmem, vmem],
        out_shape=[out, out],
        scratch_shapes=[pltpu.VMEM((SEQS * rank, 2 * rank), jnp.float32)],
        compiler_params=pltpu.CompilerParams(vmem_limit_bytes=VMEM // 4),
        name="product",
    )(edges, scale, *terms)


def shards(devices, activations, out_grads, proj_in, proj_out, seg_ids, queries):
    bits = devices.bit_length() - 1
    last = bits - 1
    rank = proj_in.shape[1]
    tokens = activations.shape[0]
    own = tokens // devices
    me = lax.axis_index("tp")

    def exchange(value, mask):
        return lax.ppermute(value, "tp", [(i, i ^ mask) for i in range(devices)])

    def swap(value, bit):
        return exchange(value, 1 << bit)

    edges = jnp.sum(
        (seg_ids[None, :] < jnp.arange(SEQS + 1, dtype=jnp.int32)[:, None]).astype(jnp.int32), axis=1
    )
    scale = 1.0 / (edges[1:] - edges[:-1]).astype(jnp.float32)

    shares = tuple(own * share // UNITS for share in CHUNKS)
    chunks = len(shares)
    on_both = [k >= chunks - BOTH_SIDES for k in range(chunks)]
    weights = jnp.concatenate([proj_in.T, proj_out.T], axis=1)
    halves = list(project(bits, 0, shares[:CUT], activations, out_grads, weights))
    sends, keeps = halves[0::2], halves[1::2]

    def route(k):
        return [0, 2, 1, *range(3, bits)] if k in CROSSED else list(range(bits))

    def turn(k, stage):
        if stage == 0:
            return 0.0 if k < CUT else 0.5
        return 0.4 if stage == 1 and k < EARLY else float(k // PAIR + stage)

    def split(value, left, b):
        shape = (1 << left.index(b), 2, -1, value.shape[1])
        parts = value.reshape(shape)
        return parts[:, 1].reshape(-1, value.shape[1]), parts[:, 0].reshape(-1, value.shape[1])

    moves = sorted(
        ((k, stage) for k in range(chunks) for stage in range(bits)),
        key=lambda move: (turn(*move), move[1], move[0]),
    )
    remaining = [list(range(1, bits)) for _ in range(chunks)]
    latest = None
    for k, stage in moves:
        b = route(k)[stage]
        if len(sends) < chunks and stage == 1:
            weights, _ = lax.optimization_barrier((weights, sends))
            halves = list(project(bits, sum(shares[:CUT]), shares[CUT:], activations, out_grads, weights))
            sends, keeps = sends + halves[0::2], keeps + halves[1::2]
        send, keep = sends[k], keeps[k]
        if b == last and not BOTH_SIDES:
            joined = [j for j in range(chunks) if j // JOIN == k // JOIN]
            if k == joined[-1]:
                send = jnp.concatenate([sends[j] for j in joined], axis=0)
                received, _ = lax.optimization_barrier((swap(send, b), latest))
                row = 0
                for j in joined:
                    keeps[j] = latest = keeps[j] + received[row : row + sends[j].shape[0]]
                    row += sends[j].shape[0]
            continue
        both = b == last and on_both[k]
        received = swap(jnp.concatenate([send, keep], axis=0) if both else send, b)
        if latest is not None:
            received, _ = lax.optimization_barrier((received, latest))
        if both:
            keeps[k] = latest = jnp.concatenate([keep, send], axis=0) + received
        elif b == last:
            keeps[k] = latest = keep + received
        else:
            following = route(k)[stage + 1]
            old, new = split(keep, remaining[k], following), split(received, remaining[k], following)
            remaining[k].remove(following)
            sends[k] = latest = old[0] + new[0]
            keeps[k] = old[1] + new[1]
    pieces = [(sum(shares[:k]), shares[k], 2 if on_both[k] else 1) for k in range(chunks)]
    early = [(keeps[k], pieces[k]) for k in range(chunks) if not on_both[k]]
    late = [(keeps[k], pieces[k]) for k in range(chunks) if on_both[k]]

    def group_product(group):
        return product(tuple(p for _, p in group), bits, own, edges, scale, [t for t, _ in group])

    send, keep = group_product(early or late)
    grads = keep + swap(send, 0)
    hops = range(1, last if late else bits)
    if early and late:
        grads = grads + swap(grads, last)
        send, keep = group_product(late)
        grads = grads + keep + swap(send, 0)
    grads = (grads + exchange(grads, 6)) + (exchange(grads, 2) + exchange(grads, 4))
    for b in hops:
        if b > 2:
            grads = grads + swap(grads, b)
    other = swap(grads, 0)
    even = (me & 1) == 0
    pair = jnp.concatenate([jnp.where(even, grads, other), jnp.where(even, other, grads)], axis=0)
    return jnp.dot(
        pair.reshape(SEQS, rank * rank), queries.T, precision=lax.Precision.HIGHEST, preferred_element_type=jnp.float32
    )


def solution(mesh):
    placed = (P("grp", "tp"), P("grp", "tp"), P("tp", None), P("tp", None), P("grp"), P("tp", None))
    return jax.shard_map(
        functools.partial(shards, mesh.shape["tp"]),
        mesh=mesh,
        in_specs=placed,
        out_specs=P("grp", "tp"),
        check_vma=False,
    )
```
